512 devices in a mesh: seq: 64 (over y, z_hi, core), dp: 8 (over x, z_lo).
Axes of the slice: x: 4, y: 8, z: 8 (z_hi: 4, z_lo: 2; z = z_hi * 2 + z_lo), core: 2. Of those that a mesh axis runs over, the one named last changes fastest.
Arguments:
- inputs: bfloat16 [8, 16384, 2048], P('dp', 'seq'), may hold values from -6 to 6
- short_filters: float32 [3, 3, 2048], replicated, may hold values from -3.5 to 3.5
- long_filter: float32 [128, 128], replicated, may hold values from -2 to 2
- grad_out: bfloat16 [8, 16384, 2048], P('dp', 'seq'), may hold values from -6 to 6
Outputs:
- grad_in: bfloat16 [8, 16384, 2048], P('dp', 'seq')
- grad_short: float32 [3, 3, 2048], replicated
- grad_long: float32 [128, 128], replicated
The draws below stay inside these ranges and needn't reach their ends.
All inputs are finite; a program needn't handle non-finite values.
Results may differ from the reference program's by a relative error of at most 0.0058.
Values may be sent and summed in bfloat16 or wider, within the bound.
No kernel may reach another device: no remote copies, remote signals or barrier semaphores. Data moves between devices by JAX's collectives and lax.ppermute only.
A program may use at most 192 MiB of HBM per device.

```python
import math
import jax
import jax.numpy as jnp
from jax import lax

C = 2048
GROUP_SIZE = 16
GROUPS = 128
TAPS = 128
BATCH = 8
LENGTH = 16384


def draw_long_filter(key, part):
    key = jax.random.fold_in(key, 7)
    reach_key, rough_key = jax.random.split(key)
    lag_steps = jnp.arange(TAPS).astype(jnp.float32)
    reach_scale = jnp.exp(jax.random.uniform(reach_key, (GROUPS, 1), jnp.float32, math.log(6.0), math.log(400.0)))
    rough_part = jnp.clip(jax.random.normal(rough_key, (GROUPS, TAPS), jnp.float32), -3.5, 3.5)
    decay_ratio = jnp.exp(-2.0 / reach_scale)
    energy = (1.0 - decay_ratio ** TAPS) / (1.0 - decay_ratio)
    return rough_part * jnp.exp(-lag_steps / reach_scale) / jnp.sqrt(energy)


def shard_levels(key, dims, cuts, least, high):
    factor_of = 1.0
    for position, parts in cuts:
        draws = jax.random.uniform(jax.random.fold_in(jax.random.fold_in(key, 6), position), (parts,), jnp.float32, least / len(cuts), high / len(cuts))
        factor_of = factor_of * jnp.repeat(jnp.exp(draws), dims[position] // parts).reshape((-1,) + (1,) * (len(dims) - 1 - position))
    return factor_of


def centred(stream_key, extent, deviation, limit, cuts=(), kind=jnp.bfloat16):
    values = deviation * jax.random.normal(stream_key, extent, jnp.float32)
    if cuts:
        values = values * shard_levels(stream_key, extent, cuts, -0.22, 0.18)
    return jnp.clip(values, -limit, limit).astype(kind)


def setup_inputs(seed: int = 0) -> dict:
    key_of = jax.random.split(jax.random.key(seed), 5)
    inputs = centred(key_of[0], (BATCH, LENGTH, C), 1.0, 6.0, ((0, 8), (1, 64)))
    short_filters = centred(key_of[1], (3, 3, C), 3 ** -0.5, 3.5, (), jnp.float32)
    long_filter = draw_long_filter(jax.random.fold_in(key_of[4], 71), 0)
    grad_out = centred(key_of[3], (BATCH, LENGTH, C), 1.0, 6.0, ((0, 8), (1, 64)))
    return dict(inputs=inputs, short_filters=short_filters, long_filter=long_filter, grad_out=grad_out)


def short_apply(signal, filters):
    length = signal.shape[0]
    padded = jnp.concatenate([jnp.zeros((2, signal.shape[1]), jnp.float32), signal], axis=0)
    return filters[0] * padded[2:] + filters[1] * padded[1:length + 1] + filters[2] * padded[:length]

def causal(signal, filter_cols):
    length = signal.shape[0]
    fft_size = 2 * length
    spectrum = jnp.fft.rfft(signal, fft_size, axis=0) * jnp.fft.rfft(filter_cols, fft_size, axis=0)
    return jnp.fft.irfft(spectrum, fft_size, axis=0)[:length]

def slab_grads(inputs_slab, cotangent_slab, filters, coarse):
    length = inputs_slab.shape[0]
    slab_width = inputs_slab.shape[1]
    filter_cols = jnp.repeat(coarse, GROUP_SIZE, axis=0).T
    as_float = inputs_slab.astype(jnp.float32)
    query = short_apply(as_float, filters[0])
    key_part = short_apply(as_float, filters[1])
    value_part = short_apply(as_float, filters[2])
    product = (key_part * value_part).astype(jnp.bfloat16)
    product_float = product.astype(jnp.float32)
    convolved = causal(product_float, filter_cols)
    cotangent = cotangent_slab.astype(jnp.float32)
    grad_conv = (cotangent * query).astype(jnp.bfloat16)
    grad_conv_float = grad_conv.astype(jnp.float32)
    grad_query = cotangent * convolved
    grad_prod = causal(grad_conv_float[::-1], filter_cols)[::-1]
    grad_key = grad_prod * value_part
    grad_value = grad_prod * key_part
    grad_in = (short_apply(grad_query[::-1], filters[0]) + short_apply(grad_key[::-1], filters[1]) + short_apply(grad_value[::-1], filters[2]))[::-1]
    padded = jnp.concatenate([jnp.zeros((2, slab_width), jnp.float32), as_float], axis=0)
    shifted = jnp.stack([padded[2 - lag_index:2 - lag_index + length] for lag_index in range(3)])
    grad_short = jnp.stack([lax.optimization_barrier(jnp.sum(branch[None] * shifted, axis=1)) for branch in (grad_query, grad_key, grad_value)])
    fft_size = 2 * length
    spectrum = jnp.fft.rfft(grad_conv_float, fft_size, axis=0) * jnp.conj(jnp.fft.rfft(product_float, fft_size, axis=0))
    spectrum = lax.optimization_barrier(jnp.sum(spectrum.reshape(spectrum.shape[0], slab_width // GROUP_SIZE, GROUP_SIZE), axis=2))
    grad_long = jnp.fft.irfft(spectrum, fft_size, axis=0)[:TAPS].T
    return (grad_in.astype(jnp.bfloat16), grad_short, grad_long)

def reference(inputs, short_filters, long_filter, grad_out):
    slab_width = 256 if C % 256 == 0 else C
    slab_count = C // slab_width
    coarse = lax.optimization_barrier(long_filter.astype(jnp.bfloat16)).astype(jnp.float32)
    filter_slabs = short_filters.reshape(3, 3, slab_count, slab_width).transpose(2, 0, 1, 3)
    coarse_slabs = coarse.reshape(slab_count, slab_width // GROUP_SIZE, TAPS)

    def one_sequence(operands):
        sequence, cotangent = operands
        input_slabs = sequence.reshape(LENGTH, slab_count, slab_width).transpose(1, 0, 2)
        cotangent_slabs = cotangent.reshape(LENGTH, slab_count, slab_width).transpose(1, 0, 2)
        grad_in, grad_short, grad_long = lax.map(lambda packed: slab_grads(*packed), (input_slabs, cotangent_slabs, filter_slabs, coarse_slabs))
        return (grad_in.transpose(1, 0, 2).reshape(LENGTH, C), grad_short, grad_long)
    grad_in, grad_short, grad_long = lax.map(one_sequence, (inputs, grad_out))
    grad_scale = 1.0 / math.sqrt(BATCH * LENGTH)
    grad_short = lax.optimization_barrier(jnp.sum(grad_short, axis=0)).transpose(1, 2, 0, 3).reshape(3, 3, C) * grad_scale
    grad_long = lax.optimization_barrier(jnp.sum(grad_long, axis=0)).reshape(GROUPS, TAPS) * grad_scale
    return (grad_in, grad_short, grad_long)
```

```python
import functools
import math

import jax
import jax.numpy as jnp
from jax import lax
from jax.experimental import pallas as pl
from jax.experimental.pallas import tpu as pltpu
from jax.sharding import Mesh, PartitionSpec as P

F32 = jnp.float32
BF16 = jnp.bfloat16
LANES = 128
EDGE = 16
PIECE = 32


def taps_of(filt_ref, branch, lo, hi):
    return [filt_ref[3 * branch + lag : 3 * branch + lag + 1, lo:hi] for lag in range(3)]


def shorten(taps, rows_at):
    return taps[0] * rows_at(0) + taps[1] * rows_at(1) + taps[2] * rows_at(2)


def edge_kernel(x_ref, g_ref, filt_ref, ahead_ref, behind_ref, ext):
    rows, width = x_ref.shape
    taps = ahead_ref.shape[0] - EDGE
    ext[0:8, :] = jnp.zeros((8, width), F32)
    ext[8:, :] = x_ref[...].astype(F32)
    query_taps, key_taps, value_taps = (taps_of(filt_ref, i, 0, width) for i in range(3))
    for start in range(0, taps, PIECE):
        tail = rows - taps + start
        at = lambda lag: ext[8 + tail - lag : 8 + tail - lag + PIECE, :]
        product = shorten(key_taps, at) * shorten(value_taps, at)
        ahead_ref[start : start + PIECE, :] = product.astype(BF16)
        at = lambda lag: ext[8 + start - lag : 8 + start - lag + PIECE, :]
        query = shorten(query_taps, at)
        grad = g_ref[start : start + PIECE, :].astype(F32) * query
        behind_ref[start : start + PIECE, :] = grad.astype(BF16)
    ahead_ref[taps:, :] = x_ref[rows - EDGE :, :]
    behind_ref[taps : taps + EDGE, :] = x_ref[:EDGE, :]
    behind_ref[taps + EDGE :, :] = g_ref[:EDGE, :]


def edge_call(x, g, filt, taps, width):
    rows, chans = x.shape
    whole = lambda r: pl.BlockSpec((r, width), lambda i: (0, i))
    return pl.pallas_call(
        edge_kernel,
        grid=(chans // width,),
        in_specs=[whole(rows), whole(rows), whole(filt.shape[0])],
        out_specs=[whole(taps + EDGE), whole(taps + 2 * EDGE)],
        out_shape=[
            jax.ShapeDtypeStruct((taps + EDGE, chans), BF16),
            jax.ShapeDtypeStruct((taps + 2 * EDGE, chans), BF16),
        ],
        scratch_shapes=[pltpu.VMEM((rows + 8, width), F32)],
        name="edges",
    )(x, g, filt)


def table_kernel(coarse_ref, turned_ref, fwd_ref, bwd_ref):
    taps = coarse_ref.shape[1]
    row = lax.broadcasted_iota(jnp.int32, (taps, taps), 0)
    col = lax.broadcasted_iota(jnp.int32, (taps, taps), 1)
    for j in range(coarse_ref.shape[0]):
        at = slice(j * taps, (j + 1) * taps)
        circ = jnp.broadcast_to(turned_ref[j : j + 1, :], (taps, taps))
        circ = pltpu.roll(circ, 0, 1, stride=1, stride_axis=0)
        fwd_ref[at, :taps] = jnp.where(col > row, circ, 0.0).astype(BF16)
        fwd_ref[at, taps:] = jnp.where(col <= row, circ, 0.0).astype(BF16)
        circ = jnp.broadcast_to(coarse_ref[j : j + 1, :], (taps, taps))
        circ = pltpu.roll(circ, 0, 1, stride=1, stride_axis=0)
        bwd_ref[at, :taps] = jnp.where(col >= row, circ, 0.0).astype(BF16)
        bwd_ref[at, taps:] = jnp.where(col < row, circ, 0.0).astype(BF16)


def table_call(coarse, turned, step):
    groups, taps = coarse.shape
    table = jax.ShapeDtypeStruct((groups * taps, 2 * taps), BF16)
    return pl.pallas_call(
        table_kernel,
        grid=(groups // step,),
        in_specs=[pl.BlockSpec((step, taps), lambda i: (i, 0))] * 2,
        out_specs=[pl.BlockSpec((step * taps, 2 * taps), lambda i: (i, 0))] * 2,
        out_shape=[table, table],
        cost_estimate=pl.CostEstimate(
            flops=groups * taps * taps * 40, bytes_accessed=groups * taps * taps * 8, transcendentals=0
        ),
        name="tables",
    )(coarse, turned)


def main_kernel(
    dot_groups,
    x_ref,
    g_ref,
    ahead_ref,
    behind_ref,
    filt_ref,
    fwd_ref,
    bwd_ref,
    out_ref,
    rim_ref,
    head_ref,
    packed_ref,
    ext,
    nxt,
    key_s,
    value_s,
    prod_s,
    grad_s,
    conv_s,
    back_s,
    lag1,
    lag2,
    fold,
):
    rows, width = x_ref.shape
    taps = ahead_ref.shape[0] - EDGE
    group_width = 16
    per = LANES // group_width
    pieces = range(0, rows, PIECE)
    ext[0:EDGE, :] = ahead_ref[taps:, :].astype(F32)
    ext[EDGE:, :] = x_ref[...].astype(F32)
    query_taps, key_taps, value_taps = (taps_of(filt_ref, i, 0, width) for i in range(3))
    nxt[0:8, :] = ext[EDGE + rows - 8 :, :]
    nxt[8:, :] = behind_ref[taps : taps + EDGE, :].astype(F32)
    query = shorten(query_taps, lambda lag: nxt[8 - lag : 8 - lag + EDGE, :])
    grad = behind_ref[taps + EDGE :, :].astype(F32) * query
    prod_s[0:taps, :] = ahead_ref[0:taps, :]
    grad_s[rows : rows + EDGE, :] = grad.astype(BF16)
    grad_s[rows + EDGE :, :] = behind_ref[EDGE:taps, :]
    for start in pieces:
        at = lambda lag: ext[EDGE + start - lag : EDGE + start - lag + PIECE, :]
        key, value = shorten(key_taps, at), shorten(value_taps, at)
        key_s[start : start + PIECE, :] = key
        value_s[start : start + PIECE, :] = value
        prod_s[taps + start : taps + start + PIECE, :] = (key * value).astype(BF16)
        grad = g_ref[start : start + PIECE, :].astype(F32) * shorten(query_taps, at)
        grad_s[start : start + PIECE, :] = grad.astype(BF16)
    lane = lax.broadcasted_iota(jnp.int32, (taps, 2 * LANES), 1) % LANES // group_width
    row = lax.broadcasted_iota(jnp.int32, (taps, taps), 0)
    col = lax.broadcasted_iota(jnp.int32, (taps, taps), 1)
    for sub in range(width // LANES):
        at = slice(sub * LANES, (sub + 1) * LANES)
        window = jnp.concatenate([prod_s[0 : 2 * taps, at], prod_s[taps : 3 * taps, at]], axis=1)
        after = jnp.concatenate([grad_s[0 : 2 * taps, at], grad_s[taps : 3 * taps, at]], axis=1)
        both = jnp.concatenate([grad_s[0:taps, at], grad_s[taps : 2 * taps, at]], axis=1)
        for table_ref, operand, result in ((fwd_ref, window, conv_s), (bwd_ref, after, back_s)):
            total = None
            for first in range(0, per, dot_groups):
                base = (sub * per + first) * taps
                part = jnp.dot(
                    table_ref[base : base + dot_groups * taps, :], operand, preferred_element_type=F32
                )
                for j in range(dot_groups):
                    mine = part[j * taps : (j + 1) * taps, :]
                    total = mine if total is None else jnp.where(lane == first + j, mine, total)
            result[0:taps, at] = total[:, :LANES]
            result[taps : 2 * taps, at] = total[:, LANES:]
        for first in range(0, per, dot_groups):
            masked = jnp.concatenate(
                [jnp.where(lane == first + j, both, jnp.zeros_like(both)) for j in range(dot_groups)], axis=0
            )
            moments = lax.dot_general(
                masked, window, (((1,), (1,)), ((), ())), preferred_element_type=F32
            )
            for j in range(dot_groups):
                mine = moments[j * taps : (j + 1) * taps, :]
                part = jnp.where(col <= row, mine[:, taps:], mine[:, :taps])
                half = taps // 2
                while half >= 8:
                    part = part[:half] + pltpu.roll(part[half:], taps - half, 1)
                    half //= 2
                fold[(first + j) * 8 : (first + j + 1) * 8, :] = part
        total = fold[pl.ds(0, per, stride=8), :]
        for r in range(1, 8):
            total = total + pltpu.roll(fold[pl.ds(r, per, stride=8), :], taps - r, 1)
        packed_ref[sub, 0:per, :] = total
    lag1[rows:, :] = jnp.zeros((8, width), F32)
    lag2[rows:, :] = jnp.zeros((8, width), F32)
    sums = [None] * 9
    by_lag = [[filt_ref[3 * i + lag : 3 * i + lag + 1, :] for i in range(3)] for lag in range(3)]
    for start in reversed(pieces):
        at = slice(start, start + PIECE)
        back = back_s[at, :]
        grads = (
            g_ref[at, :].astype(F32) * conv_s[at, :],
            back * value_s[at, :],
            back * key_s[at, :],
        )
        for lag in range(3):
            shifted = ext[EDGE + start - lag : EDGE + start - lag + PIECE, :]
            for i in range(3):
                term = grads[i] * shifted
                term = sum(term[r : r + 8] for r in range(0, PIECE, 8))
                sums[3 * i + lag] = term if sums[3 * i + lag] is None else sums[3 * i + lag] + term
        mixed = [sum(by_lag[lag][i] * grads[i] for i in range(3)) for lag in range(3)]
        lag1[at, :] = mixed[1]
        lag2[at, :] = mixed[2]
        total = mixed[0] + lag1[start + 1 : start + 1 + PIECE, :] + lag2[start + 2 : start + 2 + PIECE, :]
        out_ref[at, :] = total.astype(BF16)
        if start == rows - PIECE:
            rim_ref[...] = total[PIECE - 8 :, :]
    head_ref[0:1, :] = lag2[0:1, :]
    head_ref[1:2, :] = lag1[0:1, :] + lag2[1:2, :]
    head_ref[2:, :] = jnp.zeros((6, width), F32)
    for k in range(9):
        line = jnp.sum(sums[k], axis=0, keepdims=True)
        for sub in range(width // LANES):
            packed_ref[sub, per + k : per + k + 1, :] = line[:, sub * LANES : (sub + 1) * LANES]


def main_call(x, g, ahead, behind, filt, fwd, bwd, width, dot_groups):
    rows, chans = x.shape
    taps = ahead.shape[0] - EDGE
    groups = fwd.shape[0] // taps
    steps = chans // width
    per = groups // steps
    subs = width // LANES
    col = lambda r: pl.BlockSpec((r, width), lambda i: (0, i))
    table = pl.BlockSpec((per * taps, 2 * taps), lambda i: (i, 0))
    f32 = lambda *shape: jax.ShapeDtypeStruct(shape, F32)
    wide = lambda r, kind=F32: pltpu.VMEM((r, width), kind)
    return pl.pallas_call(
        functools.partial(main_kernel, dot_groups),
        grid=(steps,),
        in_specs=[
            col(rows), col(rows), col(taps + EDGE), col(taps + 2 * EDGE), col(filt.shape[0]), table, table,
        ],
        out_specs=[
            col(rows), col(8), col(8), pl.BlockSpec((subs, 17, taps), lambda i: (i, 0, 0)),
        ],
        out_shape=[
            jax.ShapeDtypeStruct((rows, chans), BF16), f32(8, chans), f32(8, chans),
            f32(steps * subs, 17, taps),
        ],
        scratch_shapes=[
            wide(rows + EDGE), wide(8 + EDGE), wide(rows), wide(rows), wide(rows + taps, BF16),
            wide(rows + taps, BF16), wide(rows), wide(rows), wide(rows + 8), wide(rows + 8),
            pltpu.VMEM((8 * LANES // 16, taps), F32),
        ],
        compiler_params=pltpu.CompilerParams(vmem_limit_bytes=48 * 1024 * 1024),
        cost_estimate=pl.CostEstimate(flops=26 * 10**9, bytes_accessed=24 * 2**20, transcendentals=0),
        name="operator",
    )(x, g, ahead, behind, filt, fwd, bwd)


def summed(part, inner, outer):
    inner_size, outer_size = lax.axis_size(inner), lax.axis_size(outer)
    shape = part.shape
    part = part.reshape((inner_size, shape[0] // inner_size) + shape[1:])
    part = jnp.sum(lax.all_to_all(part, inner, 0, 0, tiled=True), axis=0)
    part = lax.optimization_barrier(jnp.broadcast_to(part[None], (outer_size,) + part.shape))
    part = jnp.sum(lax.all_to_all(part, outer, 0, 0, tiled=True), axis=0)
    part = lax.optimization_barrier(jnp.broadcast_to(part[None], (inner_size,) + part.shape))
    return lax.all_to_all(part, inner, 0, 0, tiled=True).reshape(shape)


def local(inputs, short_filters, long_filter, grad_out):
    chans = inputs.shape[-1]
    rows = inputs.shape[1]
    groups, taps = long_filter.shape
    x, g = inputs[0], grad_out[0]
    filt = short_filters.reshape(9, chans)
    coarse = long_filter.astype(BF16).astype(F32)
    turned = jnp.roll(coarse[:, ::-1], 1, axis=1)
    size = lax.axis_size(SEQ)
    onward = [(i, i + 1) for i in range(size - 1)]
    back = [(i + 1, i) for i in range(size - 1)]
    ahead, behind = edge_call(x, g, filt, taps, min(512, chans))
    ahead = lax.ppermute(ahead, SEQ, onward)
    behind = lax.ppermute(behind, SEQ, back)
    fwd, bwd = table_call(coarse, turned, 16)
    out, rim, head, packed = main_call(x, g, ahead, behind, filt, fwd, bwd, min(512, chans), 2)
    head = lax.ppermute(head[:2], SEQ, back)
    rim = (rim[6:] + head).astype(BF16)
    out = lax.dynamic_update_slice(out, rim, (rows - 2, 0))
    total = inputs.shape[0] * rows * size * lax.axis_size(DP)
    packed = summed(packed, ("core", "x", "z_lo"), ("y", "z_hi")) * (1.0 / math.sqrt(total))
    per = groups // packed.shape[0]
    long = jnp.roll(packed[:, :per].reshape(groups, taps)[:, ::-1], 1, axis=1)
    short = jnp.swapaxes(packed[:, per:], 0, 1).reshape(3, 3, chans)
    return (out[None], short, long)


SEQ = ("y", "z_hi", "core")
DP = ("x", "z_lo")


def solution(mesh):
    fine = Mesh(mesh.devices.reshape(8, 4, 2, 4, 2), SEQ + DP)
    spec = P(DP, SEQ, None)
    return jax.shard_map(
        local, mesh=fine, in_specs=(spec, P(), P(), spec), out_specs=(spec, P(), P()), check_vma=False
    )
```

```python
import functools
import math

import jax
import jax.numpy as jnp
from jax import lax
from jax.experimental import pallas as pl
from jax.experimental.pallas import tpu as pltpu
from jax.sharding import Mesh, PartitionSpec as P

F32 = jnp.float32
BF16 = jnp.bfloat16
LANES = 128
EDGE = 16
PIECE = 32
GROUP = 16
PER = LANES // GROUP
CHUNK = 32
VMEM_LIMIT = 12 * 1024 * 1024
UNROLL = 4
EDGE_LIMIT = 4 * 1024 * 1024
TABLE_LIMIT = 4 * 1024 * 1024


def taps_of(filt_ref, branch, lo, hi):
    return [filt_ref[branch, lag : lag + 1, lo:hi] for lag in range(3)]


def shorten(taps, rows_at):
    return taps[0] * rows_at(0) + taps[1] * rows_at(1) + taps[2] * rows_at(2)


def edge_kernel(x_ref, g_ref, filt_ref, *refs):
    (x_out, g_out, filt_out), halos, ext, sem = refs[:3], refs[3:-2], refs[-2], refs[-1]
    near_ref, far_refs = halos[0], halos[1:]
    rows = x_ref.shape[0]
    taps = ext.shape[0] - 8
    width = far_refs[0].shape[1]
    first = lax.axis_index("core") == 0
    copies = [
        pltpu.make_async_copy(source, target, sem.at[k])
        for k, (source, target) in enumerate(((filt_ref, filt_out), (x_ref, x_out), (g_ref, g_out)))
    ]
    for copy in copies:
        copy.start()
    for copy in copies:
        copy.wait()
    for part, far_ref in enumerate(far_refs):

        def tile(i, _):
            there = pl.ds(pl.multiple_of(i * LANES, LANES), LANES)
            at = pl.ds(pl.multiple_of(part * width + i * LANES, LANES), LANES)

            def give(here, ahead, behind):
                near_ref[here, at] = jnp.where(first, ahead, behind)
                far_ref[here, there] = jnp.where(first, behind, ahead)

            query_taps = [filt_out[0, lag : lag + 1, at] for lag in range(3)]
            ext[0:8, :] = jnp.zeros((8, LANES), F32)
            ext[8:, :] = x_out[0:taps, at].astype(F32)
            for start in range(0, taps, PIECE):
                here = slice(start, start + PIECE)
                query = shorten(query_taps, lambda lag: ext[8 + start - lag : 8 + start - lag + PIECE, :])
                tail = rows - taps - EDGE + start
                give(
                    here,
                    x_out[tail : tail + PIECE, at],
                    (g_out[here, at].astype(F32) * query).astype(BF16),
                )
            rim = jnp.concatenate([ext[8:16, :], g_out[0:EDGE, at].astype(F32)[0:8]], axis=0)
            give(slice(taps, taps + EDGE), x_out[rows - EDGE :, at], rim.astype(BF16))
            return 0

        lax.fori_loop(0, width // LANES, tile, 0)


def edge_call(x, g, filters, taps, parts):
    chans = x.shape[1]
    halo = lambda width: jax.ShapeDtypeStruct((taps + EDGE, width), BF16)
    same = [jax.ShapeDtypeStruct(a.shape, a.dtype) for a in (x, g, filters)]
    made = pl.pallas_call(
        edge_kernel,
        in_specs=[pl.BlockSpec(memory_space=pltpu.HBM)] * 3,
        out_specs=[pl.BlockSpec(memory_space=pltpu.VMEM)] * (4 + parts),
        out_shape=same + [halo(chans)] + [halo(chans // parts)] * parts,
        scratch_shapes=[pltpu.VMEM((taps + 8, LANES), F32), pltpu.SemaphoreType.DMA((3,))],
        compiler_params=pltpu.CompilerParams(vmem_limit_bytes=EDGE_LIMIT),
        name="edges",
    )(x, g, filters)
    return made[:3], made[3], made[4:]


def table_kernel(filter_ref, fwd_ref, bwd_ref):
    taps = filter_ref.shape[1]
    row = lax.broadcasted_iota(jnp.int32, (taps, taps), 0)
    col = lax.broadcasted_iota(jnp.int32, (taps, taps), 1)
    lead = lax.broadcasted_iota(jnp.int32, (8, taps), 1)
    zero = jnp.zeros((taps, taps), BF16)
    chunks = taps // CHUNK

    def tile(sub, _):
        coarse = filter_ref[pl.ds(pl.multiple_of(sub * PER, PER), PER), :].astype(BF16).astype(F32)
        turned = jnp.take_along_axis(coarse, (taps - lead) % taps, axis=1)
        for j in range(PER):
            for out_ref, source, early, late in (
                (fwd_ref, turned, col > row, col <= row),
                (bwd_ref, coarse, col >= row, col < row),
            ):
                circ = jnp.broadcast_to(source[j : j + 1, :], (taps, taps))
                circ = pltpu.roll(circ, 0, 1, stride=1, stride_axis=0).astype(BF16)
                early, late = jnp.where(early, circ, zero), jnp.where(late, circ, zero)
                for r in range(chunks):
                    base = ((sub * chunks + r) * PER + j) * CHUNK
                    rows = pl.ds(pl.multiple_of(base, CHUNK), CHUNK)
                    here = slice(r * CHUNK, (r + 1) * CHUNK)
                    out_ref[rows, :taps] = early[here]
                    out_ref[rows, taps:] = late[here]
        return 0

    lax.fori_loop(0, filter_ref.shape[0] // PER, tile, 0, unroll=UNROLL)


def table_call(long_filter):
    groups, taps = long_filter.shape
    table = jax.ShapeDtypeStruct((groups * taps, 2 * taps), BF16)
    return pl.pallas_call(
        table_kernel,
        in_specs=[pl.BlockSpec(memory_space=pltpu.VMEM)],
        out_specs=[pl.BlockSpec(memory_space=pltpu.VMEM)] * 2,
        out_shape=[table, table],
        cost_estimate=pl.CostEstimate(
            flops=groups * taps * taps * 40, bytes_accessed=groups * taps * taps * 8, transcendentals=0
        ),
        compiler_params=pltpu.CompilerParams(vmem_limit_bytes=TABLE_LIMIT),
        name="tables",
    )(long_filter)


def main_kernel(
    cfg,
    scale,
    x_ref,
    g_ref,
    near_ref,
    far_ref,
    filt_ref,
    fwd_ref,
    bwd_ref,
    out_ref,
    rim_ref,
    head_ref,
    packed_ref,
    ext,
    key_s,
    value_s,
    prod_s,
    grad_s,
    lag0,
    lag1,
    lag2,
    fold,
):
    rows, width = x_ref.shape[0], cfg[0]
    taps = far_ref.shape[0] - EDGE
    lead = far_ref.shape[0]
    first = lax.axis_index("core") == 0
    chunks = taps // CHUNK
    subs = width // LANES
    lane = lax.broadcasted_iota(jnp.int32, (CHUNK, 2 * LANES), 1) % LANES // GROUP
    lane_all = lax.broadcasted_iota(jnp.int32, (taps, 2 * LANES), 1) % LANES // GROUP
    row = lax.broadcasted_iota(jnp.int32, (taps, taps), 0)
    col = lax.broadcasted_iota(jnp.int32, (taps, taps), 1)
    below = col <= row
    head_ref[2:, :] = jnp.zeros((6, head_ref.shape[1]), F32)

    chans = out_ref.shape[1]
    skip = cfg[1] * chans

    def lanes_of(tile):
        at = pl.multiple_of(tile * LANES, LANES)
        return pl.ds(at, LANES), pl.ds(pl.multiple_of(skip + at, LANES), LANES)

    def filters(at):
        return [[filt_ref[i, lag : lag + 1, at] for lag in range(3)] for i in range(3)]

    def gates(tile, sub):
        at, of = lanes_of(tile)
        query_taps, key_taps, value_taps = filters(of)
        near, far = near_ref[:, of], far_ref[:, at]
        ahead, behind = jnp.where(first, far, near), jnp.where(first, near, far)
        ext[sub, 0:lead, :] = ahead.astype(F32)
        ext[sub, lead : lead + rows, :] = x_ref[:, of].astype(F32)
        rim = behind[taps:].astype(F32)
        ext[sub, lead + rows :, :] = rim[0:8]
        query = shorten(
            query_taps, lambda lag: ext[sub, lead + rows - lag : lead + rows - lag + 8, :]
        )
        head = jnp.concatenate([(rim[8:] * query)[0:2], behind[0:EDGE].astype(F32)[2:]], axis=0)
        grad_s[sub, rows : rows + EDGE, :] = head.astype(BF16)
        grad_s[sub, rows + EDGE :, :] = behind[EDGE:taps]
        yield
        for start in range(-taps, rows, PIECE):
            base = lead + start
            lagged = [ext[sub, base - lag : base - lag + PIECE, :] for lag in range(3)]
            key, value = (shorten(t, lambda lag: lagged[lag]) for t in (key_taps, value_taps))
            prod_s[sub, taps + start : taps + start + PIECE, :] = (key * value).astype(BF16)
            if start >= 0:
                here = slice(start, start + PIECE)
                key_s[sub, here, :] = key
                value_s[sub, here, :] = value
                query = shorten(query_taps, lambda lag: lagged[lag])
                grad_s[sub, here, :] = (g_ref[here, of].astype(F32) * query).astype(BF16)
            yield

    def work(tile, sub):
        at, of = lanes_of(tile)
        taken = filters(of)
        window = jnp.concatenate([prod_s[sub, 0 : 2 * taps, :], prod_s[sub, taps:, :]], axis=1)
        after = jnp.concatenate([grad_s[sub, 0 : 2 * taps, :], grad_s[sub, taps:, :]], axis=1)
        both = jnp.concatenate([grad_s[sub, 0:taps, :], grad_s[sub, taps : 2 * taps, :]], axis=1)
        sums = [jnp.zeros((8, LANES), F32) for _ in range(9)]
        span = PER * CHUNK

        def picked(table_ref, operand, r):
            base = pl.multiple_of(((skip // LANES + tile) * chunks + r) * span, span)
            part = jnp.dot(table_ref[pl.ds(base, span), :], operand, preferred_element_type=F32)
            total = part[0:CHUNK]
            for j in range(1, PER):
                total = jnp.where(lane == j, part[j * CHUNK : (j + 1) * CHUNK], total)
            return total

        each = PER // chunks
        for r in range(chunks):
            conv, back = picked(fwd_ref, window, r), picked(bwd_ref, after, r)
            yield
            for block in range(2):
                here = slice(block * taps + r * CHUNK, block * taps + (r + 1) * CHUNK)
                wide = slice(block * LANES, (block + 1) * LANES)
                grads = (
                    g_ref[here, of].astype(F32) * conv[:, wide],
                    back[:, wide] * value_s[sub, here, :],
                    back[:, wide] * key_s[sub, here, :],
                )
                for lag in range(3):
                    base = lead + here.start - lag
                    shifted = ext[sub, base : base + CHUNK, :]
                    for i in range(3):
                        term = grads[i] * shifted
                        sums[3 * i + lag] += sum(term[k : k + 8] for k in range(0, CHUNK, 8))
                for lag, keep in enumerate((lag0, lag1, lag2)):
                    keep[sub, here, :] = sum(taken[i][lag] * grads[i] for i in range(3))
                yield
            masked = jnp.concatenate(
                [
                    jnp.where(lane_all == r * each + j, both, jnp.zeros_like(both))
                    for j in range(each)
                ],
                axis=0,
            )
            moments = lax.dot_general(
                masked, window, (((1,), (1,)), ((), ())), preferred_element_type=F32
            )
            for j in range(each):
                mine = moments[j * taps : (j + 1) * taps, :]
                part = jnp.where(below, mine[:, taps:], mine[:, :taps])
                half = taps // 2
                while half >= 8:
                    part = part[:half] + pltpu.roll(part[half:], taps - half, 1)
                    half //= 2
                slot = (r * each + j) * 8
                fold[sub, slot : slot + 8, :] = part
            yield
        for k in range(9):
            line = jnp.sum(sums[k], axis=0, keepdims=True) * scale
            packed_ref[tile, PER + k : PER + k + 1, :] = line

    def finish(tile, sub):
        at, of = lanes_of(tile)
        total = fold[sub, pl.ds(0, PER, stride=8), :]
        for r in range(1, 8):
            total = total + pltpu.roll(fold[sub, pl.ds(r, PER, stride=8), :], taps - r, 1)
        turn = (taps - lax.broadcasted_iota(jnp.int32, (PER, taps), 1)) % taps
        packed_ref[tile, 0:PER, :] = jnp.take_along_axis(total, turn, axis=1) * scale
        lag1[sub, rows:, :] = jnp.zeros((8, LANES), F32)
        lag2[sub, rows:, :] = jnp.zeros((8, LANES), F32)
        yield
        for start in range(0, rows, PIECE):
            here = slice(start, start + PIECE)
            total = (
                lag0[sub, here, :]
                + lag1[sub, start + 1 : start + 1 + PIECE, :]
                + lag2[sub, start + 2 : start + 2 + PIECE, :]
            )
            out_ref[here, at] = total.astype(BF16)
            if start == rows - PIECE:
                rim_ref[:, at] = total[PIECE - 8 :, :]
            yield
        head_ref[0:1, at] = lag2[sub, 0:1, :]
        head_ref[1:2, at] = lag1[sub, 0:1, :] + lag2[sub, 1:2, :]

    tiles = chans // LANES

    def drain(*others):
        for other in others:
            for _ in other:
                pass

    def turn(step, _):
        for sub in range(subs):
            tile = step * subs + sub
            beside = (
                gates(jnp.minimum(tile + 1, tiles - 1), (sub + 1) % subs),
                finish(jnp.maximum(tile - 1, 0), (sub - 1) % subs),
            )
            for _ in work(tile, sub):
                for other in beside:
                    next(other, None)
            drain(*beside)
        return 0

    drain(gates(0, 0))
    lax.fori_loop(0, tiles // subs, turn, 0)
    drain(finish(tiles - 1, subs - 1))


def main_call(x, g, near, far, filters, fwd, bwd, width, scale, part):
    rows, chans = x.shape[0], far.shape[1]
    lead, taps = far.shape[0], far.shape[0] - EDGE
    width = min(width, chans)
    subs = width // LANES
    f32 = lambda *shape: jax.ShapeDtypeStruct(shape, F32)
    wide = lambda r, kind=F32: pltpu.VMEM((subs, r, LANES), kind)
    return pl.pallas_call(
        functools.partial(main_kernel, (width, part, CHUNK, PIECE), scale),
        in_specs=[pl.BlockSpec(memory_space=pltpu.VMEM)] * 7,
        out_specs=[pl.BlockSpec(memory_space=pltpu.VMEM)] * 4,
        out_shape=[
            jax.ShapeDtypeStruct((rows, chans), BF16), f32(8, chans), f32(8, chans),
            f32(chans // LANES, PER + 9, taps),
        ],
        scratch_shapes=[
            wide(lead + rows + 8), wide(rows), wide(rows), wide(rows + taps, BF16),
            wide(rows + taps, BF16), wide(rows), wide(rows + 8), wide(rows + 8), wide(8 * PER),
        ],
        compiler_params=pltpu.CompilerParams(vmem_limit_bytes=VMEM_LIMIT),
        cost_estimate=pl.CostEstimate(flops=26 * 10**9, bytes_accessed=24 * 2**20, transcendentals=0),
        name="operator",
    )(x, g, near, far, filters, fwd, bwd)


def unpack_kernel(part_ref, short_ref, long_ref):
    rows = PER + 9
    for tile in range(part_ref.shape[0] // rows):
        base = tile * rows
        long_ref[tile * PER : (tile + 1) * PER, :] = part_ref[base : base + PER, :]
        for k in range(9):
            at = base + PER + k
            short_ref[k // 3, k % 3 : k % 3 + 1, tile * LANES : (tile + 1) * LANES] = part_ref[at : at + 1, :]


def on_vmem(kernel, name, out, *operands):
    return pl.pallas_call(
        kernel,
        in_specs=[pl.BlockSpec(memory_space=pltpu.VMEM)] * len(operands),
        out_specs=jax.tree.map(lambda _: pl.BlockSpec(memory_space=pltpu.VMEM), out),
        out_shape=out,
        compiler_params=pltpu.CompilerParams(vmem_limit_bytes=TABLE_LIMIT),
        name=name,
    )(*operands)


def summed(part, inner, outer):
    inner_size, outer_size = lax.axis_size(inner), lax.axis_size(outer)
    shape = part.shape
    part = part.reshape((inner_size, shape[0] // inner_size) + shape[1:])
    part = jnp.sum(lax.all_to_all(part, inner, 0, 0, tiled=True), axis=0)
    part = lax.optimization_barrier(jnp.broadcast_to(part[None], (outer_size,) + part.shape))
    part = jnp.sum(lax.all_to_all(part, outer, 0, 0, tiled=True), axis=0)
    part = lax.optimization_barrier(jnp.broadcast_to(part[None], (inner_size,) + part.shape))
    return lax.all_to_all(part, inner, 0, 0, tiled=True).reshape(shape)


PARTS = 2
WIDTH = 1024


def local(inputs, short_filters, long_filter, grad_out):
    chans = inputs.shape[-1]
    rows = inputs.shape[1]
    groups, taps = long_filter.shape
    x, g = inputs[0], grad_out[0]
    size = lax.axis_size(SEQ)
    within = [(i, i ^ 1) for i in range(size)]
    between = [(i, i + 1) for i in range(1, size - 1, 2)] + [(i + 1, i) for i in range(1, size - 1, 2)]
    back = [(i + 1, i) for i in range(size - 1)]
    total = inputs.shape[0] * rows * size * lax.axis_size(DP)
    scale = 1.0 / math.sqrt(total)
    (x, g, filters), near, far = edge_call(x, g, short_filters, taps, PARTS)
    near = lax.ppermute(near, SEQ, within)
    far = [lax.ppermute(rows_of, SEQ, between) for rows_of in far]
    fwd, bwd = table_call(long_filter)
    done = [
        main_call(x, g, near, far[k], filters, fwd, bwd, WIDTH, scale, k)
        for k in range(PARTS)
    ]
    out, rim, head, packed = (
        jnp.concatenate([d[i] for d in done], axis=(1, 1, 1, 0)[i]) for i in range(4)
    )
    head = lax.ppermute(head[:2], SEQ, back)
    rim = (rim[6:] + head).astype(BF16)
    out = lax.dynamic_update_slice(out, rim, (rows - 2, 0))
    packed = summed(packed, ("core", "x", "z_lo"), ("y", "z_hi"))
    short, long = on_vmem(
        unpack_kernel,
        "unpack",
        (jax.ShapeDtypeStruct((3, 3, chans), F32), jax.ShapeDtypeStruct((groups, taps), F32)),
        packed.reshape(-1, taps),
    )
    return (out[None], short, long)


SEQ = ("y", "z_hi", "core")
DP = ("x", "z_lo")
DIMS = (8, 4, 2, 4, 2)


def solution(mesh):
    fine = Mesh(mesh.devices.reshape(DIMS), SEQ + DP)
    spec = P(DP, SEQ, None)
    return jax.shard_map(
        local, mesh=fine, in_specs=(spec, P(), P(), spec), out_specs=(spec, P(), P()), check_vma=False
    )
```

```python
import functools
import math

import jax
import jax.numpy as jnp
from jax import lax
from jax.experimental import pallas as pl
from jax.experimental.pallas import tpu as pltpu
from jax.sharding import Mesh, PartitionSpec as P

F32 = jnp.float32
BF16 = jnp.bfloat16
LANES = 128
EDGE = 16
PIECE = 32
GROUP = 16
PER = LANES // GROUP
CHUNK = 32
VMEM_LIMIT = 12 * 1024 * 1024
UNROLL = 4
EDGE_LIMIT = 4 * 1024 * 1024
TABLE_LIMIT = 4 * 1024 * 1024


def taps_of(filt_ref, branch, lo, hi):
    return [filt_ref[branch, lag : lag + 1, lo:hi] for lag in range(3)]


def shorten(taps, rows_at):
    return taps[0] * rows_at(0) + taps[1] * rows_at(1) + taps[2] * rows_at(2)


def edge_kernel(x_ref, g_ref, filt_ref, *refs):
    (x_out, g_out, filt_out), halos, ext, sem = refs[:3], refs[3:-2], refs[-2], refs[-1]
    near_ref, far_refs = halos[0], halos[1:]
    rows = x_ref.shape[0]
    taps = ext.shape[0] - 8
    width = far_refs[0].shape[1]
    first = lax.axis_index("core") == 0
    copies = [
        pltpu.make_async_copy(source, target, sem.at[k])
        for k, (source, target) in enumerate(
            (
                (filt_ref, filt_out),
                (x_ref, x_out),
                (g_ref.at[0:taps], g_out.at[0:taps]),
                (g_ref.at[taps:rows], g_out.at[taps:rows]),
            )
        )
    ]
    for copy in copies:
        copy.start()
    for copy in copies[:3]:
        copy.wait()
    for part, far_ref in enumerate(far_refs):

        def tile(i, _):
            there = pl.ds(pl.multiple_of(i * LANES, LANES), LANES)
            at = pl.ds(pl.multiple_of(part * width + i * LANES, LANES), LANES)

            def give(here, ahead, behind):
                near_ref[here, at] = jnp.where(first, ahead, behind)
                far_ref[here, there] = jnp.where(first, behind, ahead)

            query_taps = [filt_out[0, lag : lag + 1, at] for lag in range(3)]
            ext[0:8, :] = jnp.zeros((8, LANES), F32)
            ext[8:, :] = x_out[0:taps, at].astype(F32)
            for start in range(0, taps, PIECE):
                here = slice(start, start + PIECE)
                query = shorten(query_taps, lambda lag: ext[8 + start - lag : 8 + start - lag + PIECE, :])
                tail = rows - taps - EDGE + start
                give(
                    here,
                    x_out[tail : tail + PIECE, at],
                    (g_out[here, at].astype(F32) * query).astype(BF16),
                )
            rim = jnp.concatenate([ext[8:16, :], g_out[0:EDGE, at].astype(F32)[0:8]], axis=0)
            give(slice(taps, taps + EDGE), x_out[rows - EDGE :, at], rim.astype(BF16))
            return 0

        lax.fori_loop(0, width // LANES, tile, 0)
    copies[3].wait()


def edge_call(x, g, filters, taps, parts):
    chans = x.shape[1]
    halo = lambda width: jax.ShapeDtypeStruct((taps + EDGE, width), BF16)
    same = [jax.ShapeDtypeStruct(a.shape, a.dtype) for a in (x, g, filters)]
    made = pl.pallas_call(
        edge_kernel,
        in_specs=[pl.BlockSpec(memory_space=pltpu.HBM)] * 3,
        out_specs=[pl.BlockSpec(memory_space=pltpu.VMEM)] * (4 + parts),
        out_shape=same + [halo(chans)] + [halo(chans // parts)] * parts,
        scratch_shapes=[pltpu.VMEM((taps + 8, LANES), F32), pltpu.SemaphoreType.DMA((4,))],
        compiler_params=pltpu.CompilerParams(vmem_limit_bytes=EDGE_LIMIT),
        name="edges",
    )(*(pltpu.with_memory_space_constraint(a, pltpu.HBM) for a in (x, g, filters)))
    return made[:3], made[3], made[4:]


def table_kernel(filter_ref, fwd_ref, bwd_ref):
    taps = filter_ref.shape[1]
    row = lax.broadcasted_iota(jnp.int32, (taps, taps), 0)
    col = lax.broadcasted_iota(jnp.int32, (taps, taps), 1)
    lead = lax.broadcasted_iota(jnp.int32, (8, taps), 1)
    zero = jnp.zeros((taps, taps), BF16)
    chunks = taps // CHUNK

    def tile(sub, _):
        coarse = filter_ref[pl.ds(pl.multiple_of(sub * PER, PER), PER), :].astype(BF16).astype(F32)
        turned = jnp.take_along_axis(coarse, (taps - lead) % taps, axis=1)
        for j in range(PER):
            for out_ref, source, early, late in (
                (fwd_ref, turned, col > row, col <= row),
                (bwd_ref, coarse, col >= row, col < row),
            ):
                circ = jnp.broadcast_to(source[j : j + 1, :], (taps, taps))
                circ = pltpu.roll(circ, 0, 1, stride=1, stride_axis=0).astype(BF16)
                early, late = jnp.where(early, circ, zero), jnp.where(late, circ, zero)
                for r in range(chunks):
                    base = ((sub * chunks + r) * PER + j) * CHUNK
                    rows = pl.ds(pl.multiple_of(base, CHUNK), CHUNK)
                    here = slice(r * CHUNK, (r + 1) * CHUNK)
                    out_ref[rows, :taps] = early[here]
                    out_ref[rows, taps:] = late[here]
        return 0

    lax.fori_loop(0, filter_ref.shape[0] // PER, tile, 0, unroll=UNROLL)


def table_call(long_filter):
    groups, taps = long_filter.shape
    table = jax.ShapeDtypeStruct((groups * taps, 2 * taps), BF16)
    return pl.pallas_call(
        table_kernel,
        in_specs=[pl.BlockSpec(memory_space=pltpu.VMEM)],
        out_specs=[pl.BlockSpec(memory_space=pltpu.VMEM)] * 2,
        out_shape=[table, table],
        cost_estimate=pl.CostEstimate(
            flops=groups * taps * taps * 40, bytes_accessed=groups * taps * taps * 8, transcendentals=0
        ),
        compiler_params=pltpu.CompilerParams(vmem_limit_bytes=TABLE_LIMIT),
        name="tables",
    )(long_filter)


def main_kernel(
    cfg,
    scale,
    x_ref,
    g_ref,
    near_ref,
    far_ref,
    filt_ref,
    fwd_ref,
    bwd_ref,
    out_ref,
    rim_ref,
    head_ref,
    packed_ref,
    ext,
    key_s,
    value_s,
    prod_s,
    grad_s,
    lag0,
    lag1,
    lag2,
    fold,
):
    rows, width = x_ref.shape[0], cfg[0]
    taps = far_ref.shape[0] - EDGE
    lead = far_ref.shape[0]
    first = lax.axis_index("core") == 0
    chunks = taps // CHUNK
    subs = width // LANES
    lane = lax.broadcasted_iota(jnp.int32, (CHUNK, 2 * LANES), 1) % LANES // GROUP
    lane_all = lax.broadcasted_iota(jnp.int32, (taps, 2 * LANES), 1) % LANES // GROUP
    row = lax.broadcasted_iota(jnp.int32, (taps, taps), 0)
    col = lax.broadcasted_iota(jnp.int32, (taps, taps), 1)
    below = col <= row
    head_ref[2:, :] = jnp.zeros((6, head_ref.shape[1]), F32)

    chans = out_ref.shape[1]
    skip = cfg[1] * chans

    def lanes_of(tile):
        at = pl.multiple_of(tile * LANES, LANES)
        return pl.ds(at, LANES), pl.ds(pl.multiple_of(skip + at, LANES), LANES)

    def filters(at):
        return [[filt_ref[i, lag : lag + 1, at] for lag in range(3)] for i in range(3)]

    def gates(tile, sub):
        at, of = lanes_of(tile)
        query_taps, key_taps, value_taps = filters(of)
        near, far = near_ref[:, of], far_ref[:, at]
        ahead, behind = jnp.where(first, far, near), jnp.where(first, near, far)
        ext[sub, 0:lead, :] = ahead.astype(F32)
        ext[sub, lead : lead + rows, :] = x_ref[:, of].astype(F32)
        rim = behind[taps:].astype(F32)
        ext[sub, lead + rows :, :] = rim[0:8]
        query = shorten(
            query_taps, lambda lag: ext[sub, lead + rows - lag : lead + rows - lag + 8, :]
        )
        head = jnp.concatenate([(rim[8:] * query)[0:2], behind[0:EDGE].astype(F32)[2:]], axis=0)
        grad_s[sub, rows : rows + EDGE, :] = head.astype(BF16)
        grad_s[sub, rows + EDGE :, :] = behind[EDGE:taps]
        yield
        for start in range(-taps, rows, PIECE):
            base = lead + start
            lagged = [ext[sub, base - lag : base - lag + PIECE, :] for lag in range(3)]
            key, value = (shorten(t, lambda lag: lagged[lag]) for t in (key_taps, value_taps))
            prod_s[sub, taps + start : taps + start + PIECE, :] = (key * value).astype(BF16)
            if start >= 0:
                here = slice(start, start + PIECE)
                key_s[sub, here, :] = key
                value_s[sub, here, :] = value
                query = shorten(query_taps, lambda lag: lagged[lag])
                grad_s[sub, here, :] = (g_ref[here, of].astype(F32) * query).astype(BF16)
            yield

    def work(tile, sub):
        at, of = lanes_of(tile)
        taken = filters(of)
        window = jnp.concatenate([prod_s[sub, 0 : 2 * taps, :], prod_s[sub, taps:, :]], axis=1)
        after = jnp.concatenate([grad_s[sub, 0 : 2 * taps, :], grad_s[sub, taps:, :]], axis=1)
        both = jnp.concatenate([grad_s[sub, 0:taps, :], grad_s[sub, taps : 2 * taps, :]], axis=1)
        sums = [jnp.zeros((8, LANES), F32) for _ in range(9)]
        span = PER * CHUNK

        def picked(table_ref, operand, r):
            base = pl.multiple_of(((skip // LANES + tile) * chunks + r) * span, span)
            part = jnp.dot(table_ref[pl.ds(base, span), :], operand, preferred_element_type=F32)
            total = part[0:CHUNK]
            for j in range(1, PER):
                total = jnp.where(lane == j, part[j * CHUNK : (j + 1) * CHUNK], total)
            return total

        each = PER // chunks
        for r in range(chunks):
            conv, back = picked(fwd_ref, window, r), picked(bwd_ref, after, r)
            yield
            for block in range(2):
                here = slice(block * taps + r * CHUNK, block * taps + (r + 1) * CHUNK)
                wide = slice(block * LANES, (block + 1) * LANES)
                grads = (
                    g_ref[here, of].astype(F32) * conv[:, wide],
                    back[:, wide] * value_s[sub, here, :],
                    back[:, wide] * key_s[sub, here, :],
                )
                for lag in range(3):
                    base = lead + here.start - lag
                    shifted = ext[sub, base : base + CHUNK, :]
                    for i in range(3):
                        term = grads[i] * shifted
                        sums[3 * i + lag] += sum(term[k : k + 8] for k in range(0, CHUNK, 8))
                for lag, keep in enumerate((lag0, lag1, lag2)):
                    keep[sub, here, :] = sum(taken[i][lag] * grads[i] for i in range(3))
                yield
            masked = jnp.concatenate(
                [
                    jnp.where(lane_all == r * each + j, both, jnp.zeros_like(both))
                    for j in range(each)
                ],
                axis=0,
            )
            moments = lax.dot_general(
                masked, window, (((1,), (1,)), ((), ())), preferred_element_type=F32
            )
            for j in range(each):
                mine = moments[j * taps : (j + 1) * taps, :]
                part = jnp.where(below, mine[:, taps:], mine[:, :taps])
                half = taps // 2
                while half >= 8:
                    part = part[:half] + pltpu.roll(part[half:], taps - half, 1)
                    half //= 2
                slot = (r * each + j) * 8
                fold[sub, slot : slot + 8, :] = part
            yield
        for k in range(9):
            line = jnp.sum(sums[k], axis=0, keepdims=True) * scale
            packed_ref[tile, PER + k : PER + k + 1, :] = line

    def finish(tile, sub):
        at, of = lanes_of(tile)
        total = fold[sub, pl.ds(0, PER, stride=8), :]
        for r in range(1, 8):
            total = total + pltpu.roll(fold[sub, pl.ds(r, PER, stride=8), :], taps - r, 1)
        turn = (taps - lax.broadcasted_iota(jnp.int32, (PER, taps), 1)) % taps
        packed_ref[tile, 0:PER, :] = jnp.take_along_axis(total, turn, axis=1) * scale
        lag1[sub, rows:, :] = jnp.zeros((8, LANES), F32)
        lag2[sub, rows:, :] = jnp.zeros((8, LANES), F32)
        yield
        for start in range(0, rows, PIECE):
            here = slice(start, start + PIECE)
            total = (
                lag0[sub, here, :]
                + lag1[sub, start + 1 : start + 1 + PIECE, :]
                + lag2[sub, start + 2 : start + 2 + PIECE, :]
            )
            out_ref[here, at] = total.astype(BF16)
            if start == rows - PIECE:
                rim_ref[:, at] = total[PIECE - 8 :, :]
            yield
        head_ref[0:1, at] = lag2[sub, 0:1, :]
        head_ref[1:2, at] = lag1[sub, 0:1, :] + lag2[sub, 1:2, :]

    tiles = chans // LANES

    def drain(*others):
        for other in others:
            for _ in other:
                pass

    def turn(step, _):
        for sub in range(subs):
            tile = step * subs + sub
            beside = (
                gates(jnp.minimum(tile + 1, tiles - 1), (sub + 1) % subs),
                finish(jnp.maximum(tile - 1, 0), (sub - 1) % subs),
            )
            for _ in work(tile, sub):
                for other in beside:
                    next(other, None)
            drain(*beside)
        return 0

    drain(gates(0, 0))
    lax.fori_loop(0, tiles // subs, turn, 0)
    drain(finish(tiles - 1, subs - 1))


def main_call(x, g, near, far, filters, fwd, bwd, width, scale, part):
    rows, chans = x.shape[0], far.shape[1]
    lead, taps = far.shape[0], far.shape[0] - EDGE
    width = min(width, chans)
    subs = width // LANES
    f32 = lambda *shape: jax.ShapeDtypeStruct(shape, F32)
    wide = lambda r, kind=F32: pltpu.VMEM((subs, r, LANES), kind)
    return pl.pallas_call(
        functools.partial(main_kernel, (width, part, CHUNK, PIECE), scale),
        in_specs=[pl.BlockSpec(memory_space=pltpu.VMEM)] * 7,
        out_specs=[pl.BlockSpec(memory_space=pltpu.VMEM)] * 4,
        out_shape=[
            jax.ShapeDtypeStruct((rows, chans), BF16), f32(8, chans), f32(8, chans),
            f32(chans // LANES, PER + 9, taps),
        ],
        scratch_shapes=[
            wide(lead + rows + 8), wide(rows), wide(rows), wide(rows + taps, BF16),
            wide(rows + taps, BF16), wide(rows), wide(rows + 8), wide(rows + 8), wide(8 * PER),
        ],
        compiler_params=pltpu.CompilerParams(vmem_limit_bytes=VMEM_LIMIT),
        cost_estimate=pl.CostEstimate(flops=26 * 10**9, bytes_accessed=24 * 2**20, transcendentals=0),
        name="operator",
    )(x, g, near, far, filters, fwd, bwd)


def spread_kernel(part_ref, all_ref):
    rows = PER + 9
    parts = [part_ref[k : k + rows, :] for k in range(0, part_ref.shape[0], rows)]
    while len(parts) > 1:
        parts = [a + b for a, b in zip(parts[::2], parts[1::2])]
    for k in range(0, all_ref.shape[0], rows):
        all_ref[k : k + rows, :] = parts[0]


def unpack_kernel(part_ref, short_ref, long_ref):
    rows = PER + 9
    for tile in range(part_ref.shape[0] // rows):
        base = tile * rows
        long_ref[tile * PER : (tile + 1) * PER, :] = part_ref[base : base + PER, :]
        for k in range(9):
            at = base + PER + k
            short_ref[k // 3, k % 3 : k % 3 + 1, tile * LANES : (tile + 1) * LANES] = part_ref[at : at + 1, :]


def on_vmem(kernel, name, out, *operands):
    return pl.pallas_call(
        kernel,
        in_specs=[pl.BlockSpec(memory_space=pltpu.VMEM)] * len(operands),
        out_specs=jax.tree.map(lambda _: pl.BlockSpec(memory_space=pltpu.VMEM), out),
        out_shape=out,
        compiler_params=pltpu.CompilerParams(vmem_limit_bytes=TABLE_LIMIT),
        name=name,
    )(*operands)


def summed(part, inner, outer):
    rows, lanes = part.shape[1:]
    inner_size, outer_size = lax.axis_size(inner), lax.axis_size(outer)
    copies = lambda n: jax.ShapeDtypeStruct((n * rows, lanes), F32)
    swap = lambda a, axes, n: lax.all_to_all(a.reshape(n, -1, rows, lanes), axes, 0, 0, tiled=True)
    part = swap(part, inner, inner_size).reshape(-1, lanes)
    part = on_vmem(spread_kernel, "sum_inner", copies(outer_size), part)
    part = swap(part, outer, outer_size).reshape(-1, lanes)
    part = on_vmem(spread_kernel, "sum_outer", copies(inner_size), part)
    return swap(part, inner, inner_size)


PARTS = 2
WIDTH = 1024


def local(inputs, short_filters, long_filter, grad_out):
    chans = inputs.shape[-1]
    rows = inputs.shape[1]
    groups, taps = long_filter.shape
    x, g = inputs[0], grad_out[0]
    size = lax.axis_size(SEQ)
    within = [(i, i ^ 1) for i in range(size)]
    between = [(i, i + 1) for i in range(1, size - 1, 2)] + [(i + 1, i) for i in range(1, size - 1, 2)]
    back = [(i + 1, i) for i in range(size - 1)]
    total = inputs.shape[0] * rows * size * lax.axis_size(DP)
    scale = 1.0 / math.sqrt(total)
    (x, g, filters), near, far = edge_call(x, g, short_filters, taps, PARTS)
    near = lax.ppermute(near, SEQ, within)
    far = [lax.ppermute(rows_of, SEQ, between) for rows_of in far]
    fwd, bwd = table_call(long_filter)
    done = [
        main_call(x, g, near, far[k], filters, fwd, bwd, WIDTH, scale, k)
        for k in range(PARTS)
    ]
    out, rim, head, packed = (
        jnp.concatenate([d[i] for d in done], axis=(1, 1, 1, 0)[i]) for i in range(4)
    )
    head = lax.ppermute(head[:2], SEQ, back)
    rim = (rim[6:] + head).astype(BF16)
    out = lax.dynamic_update_slice(out, rim, (rows - 2, 0))
    packed = summed(packed, ("core", "x", "z_lo"), ("y", "z_hi"))
    short, long = on_vmem(
        unpack_kernel,
        "unpack",
        (jax.ShapeDtypeStruct((3, 3, chans), F32), jax.ShapeDtypeStruct((groups, taps), F32)),
        packed.reshape(-1, taps),
    )
    return (out[None], short, long)


SEQ = ("y", "z_hi", "core")
DP = ("x", "z_lo")
DIMS = (8, 4, 2, 4, 2)


def solution(mesh):
    fine = Mesh(mesh.devices.reshape(DIMS), SEQ + DP)
    spec = P(DP, SEQ, None)
    return jax.shard_map(
        local, mesh=fine, in_specs=(spec, P(), P(), spec), out_specs=(spec, P(), P()), check_vma=False
    )
```

```python
import functools
import math

import jax
import jax.numpy as jnp
from jax import lax
from jax.experimental import pallas as pl
from jax.experimental.pallas import tpu as pltpu
from jax.sharding import Mesh, PartitionSpec as P

F32 = jnp.float32
BF16 = jnp.bfloat16
LANES = 128
EDGE = 16
PIECE = 32
GROUP = 16
PER = LANES // GROUP
CHUNK = 32
VMEM_LIMIT = 12 * 1024 * 1024
UNROLL = 4
EDGE_LIMIT = 4 * 1024 * 1024
TABLE_LIMIT = 4 * 1024 * 1024


def taps_of(filt_ref, branch, lo, hi):
    return [filt_ref[branch, lag : lag + 1, lo:hi] for lag in range(3)]


def shorten(taps, rows_at):
    return taps[0] * rows_at(0) + taps[1] * rows_at(1) + taps[2] * rows_at(2)


def edge_kernel(x_ref, g_ref, filt_ref, *refs):
    (x_out, g_out, filt_out), halos, ext, sem = refs[:3], refs[3:-2], refs[-2], refs[-1]
    near_ref, far_refs = halos[0], halos[1:]
    rows = x_ref.shape[0]
    taps = ext.shape[0] - 8
    width = far_refs[0].shape[1]
    first = lax.axis_index("core") == 0
    copies = [
        pltpu.make_async_copy(source, target, sem.at[k])
        for k, (source, target) in enumerate(
            (
                (filt_ref, filt_out),
                (x_ref, x_out),
                (g_ref.at[0:taps], g_out.at[0:taps]),
                (g_ref.at[taps:rows], g_out.at[taps:rows]),
            )
        )
    ]
    for copy in copies:
        copy.start()
    for copy in copies[:3]:
        copy.wait()
    for part, far_ref in enumerate(far_refs):

        def tile(i, _):
            there = pl.ds(pl.multiple_of(i * LANES, LANES), LANES)
            at = pl.ds(pl.multiple_of(part * width + i * LANES, LANES), LANES)

            def give(here, ahead, behind):
                near_ref[here, at] = jnp.where(first, ahead, behind)
                far_ref[here, there] = jnp.where(first, behind, ahead)

            query_taps = [filt_out[0, lag : lag + 1, at] for lag in range(3)]
            ext[0:8, :] = jnp.zeros((8, LANES), F32)
            ext[8:, :] = x_out[0:taps, at].astype(F32)
            for start in range(0, taps, PIECE):
                here = slice(start, start + PIECE)
                query = shorten(query_taps, lambda lag: ext[8 + start - lag : 8 + start - lag + PIECE, :])
                tail = rows - taps - EDGE + start
                give(
                    here,
                    x_out[tail : tail + PIECE, at],
                    (g_out[here, at].astype(F32) * query).astype(BF16),
                )
            rim = jnp.concatenate([ext[8:16, :], g_out[0:EDGE, at].astype(F32)[0:8]], axis=0)
            give(slice(taps, taps + EDGE), x_out[rows - EDGE :, at], rim.astype(BF16))
            return 0

        lax.fori_loop(0, width // LANES, tile, 0)
    copies[3].wait()


def edge_call(x, g, filters, taps, parts):
    chans = x.shape[1]
    halo = lambda width: jax.ShapeDtypeStruct((taps + EDGE, width), BF16)
    same = [jax.ShapeDtypeStruct(a.shape, a.dtype) for a in (x, g, filters)]
    made = pl.pallas_call(
        edge_kernel,
        in_specs=[pl.BlockSpec(memory_space=pltpu.HBM)] * 3,
        out_specs=[pl.BlockSpec(memory_space=pltpu.VMEM)] * (4 + parts),
        out_shape=same + [halo(chans)] + [halo(chans // parts)] * parts,
        scratch_shapes=[pltpu.VMEM((taps + 8, LANES), F32), pltpu.SemaphoreType.DMA((4,))],
        compiler_params=pltpu.CompilerParams(vmem_limit_bytes=EDGE_LIMIT),
        name="edges",
    )(*(pltpu.with_memory_space_constraint(a, pltpu.HBM) for a in (x, g, filters)))
    return made[:3], made[3], made[4:]


def table_kernel(filter_ref, fwd_ref, bwd_ref):
    taps = filter_ref.shape[1]
    row = lax.broadcasted_iota(jnp.int32, (taps, taps), 0)
    col = lax.broadcasted_iota(jnp.int32, (taps, taps), 1)
    lead = lax.broadcasted_iota(jnp.int32, (8, taps), 1)
    zero = jnp.zeros((taps, taps), BF16)
    chunks = taps // CHUNK

    def tile(sub, _):
        coarse = filter_ref[pl.ds(pl.multiple_of(sub * PER, PER), PER), :].astype(BF16).astype(F32)
        turned = jnp.take_along_axis(coarse, (taps - lead) % taps, axis=1)
        for j in range(PER):
            for out_ref, source, early, late in (
                (fwd_ref, turned, col > row, col <= row),
                (bwd_ref, coarse, col >= row, col < row),
            ):
                circ = jnp.broadcast_to(source[j : j + 1, :], (taps, taps))
                circ = pltpu.roll(circ, 0, 1, stride=1, stride_axis=0).astype(BF16)
                early, late = jnp.where(early, circ, zero), jnp.where(late, circ, zero)
                for r in range(chunks):
                    base = ((sub * chunks + r) * PER + j) * CHUNK
                    rows = pl.ds(pl.multiple_of(base, CHUNK), CHUNK)
                    here = slice(r * CHUNK, (r + 1) * CHUNK)
                    out_ref[rows, :taps] = early[here]
                    out_ref[rows, taps:] = late[here]
        return 0

    lax.fori_loop(0, filter_ref.shape[0] // PER, tile, 0, unroll=UNROLL)


def table_call(long_filter):
    groups, taps = long_filter.shape
    table = jax.ShapeDtypeStruct((groups * taps, 2 * taps), BF16)
    return pl.pallas_call(
        table_kernel,
        in_specs=[pl.BlockSpec(memory_space=pltpu.VMEM)],
        out_specs=[pl.BlockSpec(memory_space=pltpu.VMEM)] * 2,
        out_shape=[table, table],
        cost_estimate=pl.CostEstimate(
            flops=groups * taps * taps * 40, bytes_accessed=groups * taps * taps * 8, transcendentals=0
        ),
        compiler_params=pltpu.CompilerParams(vmem_limit_bytes=TABLE_LIMIT),
        name="tables",
    )(long_filter)


def main_kernel(
    cfg,
    scale,
    x_ref,
    g_ref,
    near_ref,
    far_ref,
    filt_ref,
    fwd_ref,
    bwd_ref,
    query_ref,
    key_ref,
    value_ref,
    packed_ref,
    ext,
    key_s,
    value_s,
    prod_s,
    grad_s,
    fold,
):
    rows, width = x_ref.shape[0], cfg[0]
    taps = far_ref.shape[0] - EDGE
    lead = far_ref.shape[0]
    first = lax.axis_index("core") == 0
    chunks = taps // CHUNK
    subs = width // LANES
    lane = lax.broadcasted_iota(jnp.int32, (CHUNK, 2 * LANES), 1) % LANES // GROUP
    lane_all = lax.broadcasted_iota(jnp.int32, (taps, 2 * LANES), 1) % LANES // GROUP
    row = lax.broadcasted_iota(jnp.int32, (taps, taps), 0)
    col = lax.broadcasted_iota(jnp.int32, (taps, taps), 1)
    below = col <= row
    chans = query_ref.shape[1]
    skip = cfg[1] * chans

    def lanes_of(tile):
        at = pl.multiple_of(tile * LANES, LANES)
        return pl.ds(at, LANES), pl.ds(pl.multiple_of(skip + at, LANES), LANES)

    def filters(at):
        return [[filt_ref[i, lag : lag + 1, at] for lag in range(3)] for i in range(3)]

    def gates(tile, sub):
        at, of = lanes_of(tile)
        query_taps, key_taps, value_taps = filters(of)
        near, far = near_ref[:, of], far_ref[:, at]
        ahead, behind = jnp.where(first, far, near), jnp.where(first, near, far)
        ext[sub, 0:lead, :] = ahead.astype(F32)
        ext[sub, lead : lead + rows, :] = x_ref[:, of].astype(F32)
        rim = behind[taps:].astype(F32)
        ext[sub, lead + rows :, :] = rim[0:8]
        query = shorten(
            query_taps, lambda lag: ext[sub, lead + rows - lag : lead + rows - lag + 8, :]
        )
        head = jnp.concatenate([(rim[8:] * query)[0:2], behind[0:EDGE].astype(F32)[2:]], axis=0)
        grad_s[sub, rows : rows + EDGE, :] = head.astype(BF16)
        grad_s[sub, rows + EDGE :, :] = behind[EDGE:taps]
        yield
        for start in range(-taps, rows, PIECE):
            base = lead + start
            lagged = [ext[sub, base - lag : base - lag + PIECE, :] for lag in range(3)]
            key, value = (shorten(t, lambda lag: lagged[lag]) for t in (key_taps, value_taps))
            prod_s[sub, taps + start : taps + start + PIECE, :] = (key * value).astype(BF16)
            if start >= 0:
                here = slice(start, start + PIECE)
                key_s[sub, here, :] = key
                value_s[sub, here, :] = value
                query = shorten(query_taps, lambda lag: lagged[lag])
                grad_s[sub, here, :] = (g_ref[here, of].astype(F32) * query).astype(BF16)
            yield

    def work(tile, sub):
        at, of = lanes_of(tile)
        window = jnp.concatenate([prod_s[sub, 0 : 2 * taps, :], prod_s[sub, taps:, :]], axis=1)
        after = jnp.concatenate([grad_s[sub, 0 : 2 * taps, :], grad_s[sub, taps:, :]], axis=1)
        both = jnp.concatenate([grad_s[sub, 0:taps, :], grad_s[sub, taps : 2 * taps, :]], axis=1)
        sums = [jnp.zeros((8, LANES), F32) for _ in range(9)]
        span = PER * CHUNK

        def picked(table_ref, operand, r):
            base = pl.multiple_of(((skip // LANES + tile) * chunks + r) * span, span)
            part = jnp.dot(table_ref[pl.ds(base, span), :], operand, preferred_element_type=F32)
            total = part[0:CHUNK]
            for j in range(1, PER):
                total = jnp.where(lane == j, part[j * CHUNK : (j + 1) * CHUNK], total)
            return total

        each = PER // chunks
        for r in range(chunks):
            conv, back = picked(fwd_ref, window, r), picked(bwd_ref, after, r)
            yield
            for block in range(2):
                here = slice(block * taps + r * CHUNK, block * taps + (r + 1) * CHUNK)
                wide = slice(block * LANES, (block + 1) * LANES)
                grads = (
                    g_ref[here, of].astype(F32) * conv[:, wide],
                    back[:, wide] * value_s[sub, here, :],
                    back[:, wide] * key_s[sub, here, :],
                )
                for lag in range(3):
                    base = lead + here.start - lag
                    shifted = ext[sub, base : base + CHUNK, :]
                    for i in range(3):
                        term = grads[i] * shifted
                        sums[3 * i + lag] += sum(term[k : k + 8] for k in range(0, CHUNK, 8))
                for keep, grad in zip((query_ref, key_ref, value_ref), grads):
                    keep[here, at] = grad
                yield
            masked = jnp.concatenate(
                [
                    jnp.where(lane_all == r * each + j, both, jnp.zeros_like(both))
                    for j in range(each)
                ],
                axis=0,
            )
            moments = lax.dot_general(
                masked, window, (((1,), (1,)), ((), ())), preferred_element_type=F32
            )
            for j in range(each):
                mine = moments[j * taps : (j + 1) * taps, :]
                part = jnp.where(below, mine[:, taps:], mine[:, :taps])
                half = taps // 2
                while half >= 8:
                    part = part[:half] + pltpu.roll(part[half:], taps - half, 1)
                    half //= 2
                slot = (r * each + j) * 8
                fold[sub, slot : slot + 8, :] = part
            yield
        for k in range(9):
            line = jnp.sum(sums[k], axis=0, keepdims=True) * scale
            packed_ref[tile, PER + k : PER + k + 1, :] = line

    def finish(tile, sub):
        at, of = lanes_of(tile)
        total = fold[sub, pl.ds(0, PER, stride=8), :]
        for r in range(1, 8):
            total = total + pltpu.roll(fold[sub, pl.ds(r, PER, stride=8), :], taps - r, 1)
        turn = (taps - lax.broadcasted_iota(jnp.int32, (PER, taps), 1)) % taps
        packed_ref[tile, 0:PER, :] = jnp.take_along_axis(total, turn, axis=1) * scale
        yield

    tiles = chans // LANES

    def drain(*others):
        for other in others:
            for _ in other:
                pass

    def turn(step, _):
        for sub in range(subs):
            tile = step * subs + sub
            beside = (
                gates(jnp.minimum(tile + 1, tiles - 1), (sub + 1) % subs),
                finish(jnp.maximum(tile - 1, 0), (sub - 1) % subs),
            )
            for _ in work(tile, sub):
                for other in beside:
                    next(other, None)
            drain(*beside)
        return 0

    drain(gates(0, 0))
    lax.fori_loop(0, tiles // subs, turn, 0)
    drain(finish(tiles - 1, subs - 1))


def main_call(x, g, near, far, filters, fwd, bwd, width, scale, part):
    rows, chans = x.shape[0], far.shape[1]
    lead, taps = far.shape[0], far.shape[0] - EDGE
    width = min(width, chans)
    subs = width // LANES
    f32 = lambda *shape: jax.ShapeDtypeStruct(shape, F32)
    wide = lambda r, kind=F32: pltpu.VMEM((subs, r, LANES), kind)
    return pl.pallas_call(
        functools.partial(main_kernel, (width, part, CHUNK, PIECE), scale),
        in_specs=[pl.BlockSpec(memory_space=pltpu.VMEM)] * 7,
        out_specs=[pl.BlockSpec(memory_space=pltpu.VMEM)] * 4,
        out_shape=[
            f32(rows, chans), f32(rows, chans), f32(rows, chans),
            f32(chans // LANES, PER + 9, taps),
        ],
        scratch_shapes=[
            wide(lead + rows + 8), wide(rows), wide(rows), wide(rows + taps, BF16),
            wide(rows + taps, BF16), wide(8 * PER),
        ],
        compiler_params=pltpu.CompilerParams(vmem_limit_bytes=VMEM_LIMIT),
        cost_estimate=pl.CostEstimate(flops=26 * 10**9, bytes_accessed=24 * 2**20, transcendentals=0),
        name="operator",
    )(x, g, near, far, filters, fwd, bwd)


def mix_kernel(*refs):
    grads, filt_ref = refs[:-8], refs[-8]
    out_ref, rim_ref, head_ref, lag0, lag1, lag2 = refs[-6:]
    rows, width = grads[0].shape
    pieces = [slice(start, start + PIECE) for start in range(0, rows, PIECE)]
    head_ref[2:, :] = jnp.zeros((6, head_ref.shape[1]), F32)
    lag1[rows:, :] = jnp.zeros((8, LANES), F32)
    lag2[rows:, :] = jnp.zeros((8, LANES), F32)
    for part in range(len(grads) // 3):

        def tile(i, _):
            there = pl.ds(pl.multiple_of(i * LANES, LANES), LANES)
            at = pl.ds(pl.multiple_of(part * width + i * LANES, LANES), LANES)
            for here in pieces:
                branches = [ref[here, there] for ref in grads[3 * part : 3 * part + 3]]
                for lag, keep in enumerate((lag0, lag1, lag2)):
                    keep[here, :] = sum(filt_ref[k, lag : lag + 1, at] * branches[k] for k in range(3))
            for here in pieces:
                start = here.start
                total = (
                    lag0[here, :]
                    + lag1[start + 1 : start + 1 + PIECE, :]
                    + lag2[start + 2 : start + 2 + PIECE, :]
                )
                out_ref[here, at] = total.astype(BF16)
                if here is pieces[-1]:
                    rim_ref[:, at] = total[PIECE - 8 :, :]
            head_ref[0:1, at] = lag2[0:1, :]
            head_ref[1:2, at] = lag1[0:1, :] + lag2[1:2, :]
            return 0

        lax.fori_loop(0, width // LANES, tile, 0)


def mix_call(grads, filters, after):
    rows, chans = grads[0].shape[0], filters.shape[2]
    f32 = lambda *shape: jax.ShapeDtypeStruct(shape, F32)
    return pl.pallas_call(
        mix_kernel,
        in_specs=[pl.BlockSpec(memory_space=pltpu.VMEM)] * (len(grads) + 1)
        + [pl.BlockSpec(memory_space=pl.ANY)],
        out_specs=[pl.BlockSpec(memory_space=pltpu.VMEM)] * 3,
        out_shape=[jax.ShapeDtypeStruct((rows, chans), BF16), f32(8, chans), f32(8, chans)],
        scratch_shapes=[pltpu.VMEM((rows + 8, LANES), F32)] * 3,
        compiler_params=pltpu.CompilerParams(vmem_limit_bytes=TABLE_LIMIT),
        name="mix",
    )(*(pltpu.with_memory_space_constraint(a, pltpu.VMEM) for a in grads), filters, after)


def spread_kernel(part_ref, all_ref):
    rows = PER + 9
    parts = [part_ref[k : k + rows, :] for k in range(0, part_ref.shape[0], rows)]
    while len(parts) > 1:
        parts = [a + b for a, b in zip(parts[::2], parts[1::2])]
    for k in range(0, all_ref.shape[0], rows):
        all_ref[k : k + rows, :] = parts[0]


def unpack_kernel(part_ref, short_ref, long_ref):
    rows = PER + 9
    for tile in range(part_ref.shape[0] // rows):
        base = tile * rows
        long_ref[tile * PER : (tile + 1) * PER, :] = part_ref[base : base + PER, :]
        for k in range(9):
            at = base + PER + k
            short_ref[k // 3, k % 3 : k % 3 + 1, tile * LANES : (tile + 1) * LANES] = part_ref[at : at + 1, :]


def on_vmem(kernel, name, out, *operands):
    return pl.pallas_call(
        kernel,
        in_specs=[pl.BlockSpec(memory_space=pltpu.VMEM)] * len(operands),
        out_specs=jax.tree.map(lambda _: pl.BlockSpec(memory_space=pltpu.VMEM), out),
        out_shape=out,
        compiler_params=pltpu.CompilerParams(vmem_limit_bytes=TABLE_LIMIT),
        name=name,
    )(*operands)


def summed(part, inner, outer):
    rows, lanes = part.shape[1:]
    inner_size, outer_size = lax.axis_size(inner), lax.axis_size(outer)
    copies = lambda n: jax.ShapeDtypeStruct((n * rows, lanes), F32)
    swap = lambda a, axes, n: lax.all_to_all(a.reshape(n, -1, rows, lanes), axes, 0, 0, tiled=True)
    part = swap(part, inner, inner_size).reshape(-1, lanes)
    part = on_vmem(spread_kernel, "sum_inner", copies(outer_size), part)
    early = part
    part = swap(part, outer, outer_size).reshape(-1, lanes)
    part = on_vmem(spread_kernel, "sum_outer", copies(inner_size), part)
    return swap(part, inner, inner_size), early


PARTS = 2
WIDTH = 1024


def local(inputs, short_filters, long_filter, grad_out):
    chans = inputs.shape[-1]
    rows = inputs.shape[1]
    groups, taps = long_filter.shape
    x, g = inputs[0], grad_out[0]
    size = lax.axis_size(SEQ)
    within = [(i, i ^ 1) for i in range(size)]
    between = [(i, i + 1) for i in range(1, size - 1, 2)] + [(i + 1, i) for i in range(1, size - 1, 2)]
    back = [(i + 1, i) for i in range(size - 1)]
    total = inputs.shape[0] * rows * size * lax.axis_size(DP)
    scale = 1.0 / math.sqrt(total)
    (x, g, filters), near, far = edge_call(x, g, short_filters, taps, PARTS)
    near = lax.ppermute(near, SEQ, within)
    far = [lax.ppermute(rows_of, SEQ, between) for rows_of in far]
    fwd, bwd = table_call(long_filter)
    done = [
        main_call(x, g, near, far[k], filters, fwd, bwd, WIDTH, scale, k)
        for k in range(PARTS)
    ]
    packed = jnp.concatenate([d[3] for d in done], axis=0)
    packed, early = summed(packed, ("core", "x", "z_lo"), ("y", "z_hi"))
    out, rim, head = mix_call([grad for d in done for grad in d[:3]], filters, early)
    head = lax.ppermute(head[:2], SEQ, back)
    rim = (rim[6:] + head).astype(BF16)
    out = lax.dynamic_update_slice(out, rim, (rows - 2, 0))
    short, long = on_vmem(
        unpack_kernel,
        "unpack",
        (jax.ShapeDtypeStruct((3, 3, chans), F32), jax.ShapeDtypeStruct((groups, taps), F32)),
        packed.reshape(-1, taps),
    )
    return (out[None], short, long)


SEQ = ("y", "z_hi", "core")
DP = ("x", "z_lo")
DIMS = (8, 4, 2, 4, 2)


def solution(mesh):
    fine = Mesh(mesh.devices.reshape(DIMS), SEQ + DP)
    spec = P(DP, SEQ, None)
    return jax.shard_map(
        local, mesh=fine, in_specs=(spec, P(), P(), spec), out_specs=(spec, P(), P()), check_vma=False
    )
```
